256 devices in a mesh: pipe: 16 (over z, core), ep: 16 (over x, y).
Axes of the slice: x: 4, y: 4, z: 8, core: 2. Of those that a mesh axis runs over, the one named last changes fastest.
Arguments:
- fore_entry: bfloat16 [16, 2048, 3584], P('pipe', 'ep'), may hold values from -6 to 6
- fore_feed: bfloat16 [1, 2048, 3584], P(None, 'ep'), may hold values from -6 to 6
- fore_route: int32 [16, 2, 2048, 1], P('pipe', None, 'ep'), may hold values from 0 to 3; in each aligned block of 128 rows (0 to 127, 128 to 255, ..., all dimensions but the last counted through in order) at most 40 rows name the same one
- fore_gate: float32 [16, 2, 2048, 1], P('pipe', None, 'ep'), may hold values from 0.2 to 1
- back_entry: bfloat16 [16, 2048, 3584], P('pipe', 'ep'), may hold values from -6 to 6
- back_feed: bfloat16 [1, 2048, 3584], P(None, 'ep'), may hold values from -6 to 6
- back_stash: bfloat16 [16, 2, 2048, 3584], P('pipe', None, 'ep'), may hold values from -6 to 6
- back_route: int32 [16, 2, 2048, 1], P('pipe', None, 'ep'), may hold values from 0 to 3; in each aligned block of 128 rows (0 to 127, 128 to 255, ..., all dimensions but the last counted through in order) at most 40 rows name the same one
- back_gate: float32 [16, 2, 2048, 1], P('pipe', None, 'ep'), may hold values from 0.2 to 1
- w_gate: bfloat16 [16, 3584, 4096], P('pipe', None, 'ep'), may hold values from -0.09375 to 0.09375
- w_up: bfloat16 [16, 3584, 4096], P('pipe', None, 'ep'), may hold values from -0.09375 to 0.09375
- w_down: bfloat16 [16, 4096, 3584], P('pipe', 'ep'), may hold values from -0.1875 to 0.1875
Outputs:
- fore_out: bfloat16 [16, 2048, 3584], P('pipe', 'ep')
- back_out: bfloat16 [16, 2048, 3584], P('pipe', 'ep')
The draws below stay inside these ranges and needn't reach their ends.
Inputs may be any that keep to these rules, and one draw needn't show every extreme that they name: `fore_route`: A token's 1 expert differ. In every section and step, the 128 tokens of one device name one expert at most 40 times, and exactly 40 times for some expert in some of these blocks. `back_route`: A token's 1 expert differ. In every section and step, the 128 tokens of one device name one expert at most 40 times, and exactly 40 times for some expert in some of these blocks.
All inputs are finite; a program needn't handle non-finite values.
Results may differ from the reference program's by a relative error of at most 0.007.
Values may be sent and summed in bfloat16 or wider, within the bound.
No kernel may reach another device: no remote copies, remote signals or barrier semaphores. Data moves between devices by JAX's collectives and lax.ppermute only.
A program may use at most 128 MiB of HBM per device.

```python
import math
import jax
import jax.numpy as jnp
import numpy as np
from jax import lax

D = 3584
FF = 1024
EXPERTS = 4
TOP = 1
TOK_DEV = 128
W = 2
TOKENS = 2048
HID = 256
CAP = 40
N_PIPE = 16
N_EP = 16


def block_scale(key, shape, pieces, least, top_value):
    level, own = 1.0, jax.random.fold_in(key, 6)
    for dim, parts in pieces:
        heights = jnp.exp(jax.random.uniform(jax.random.fold_in(own, dim), (parts,), jnp.float32, least / len(pieces), top_value / len(pieces)))
        level = level * jnp.repeat(heights, shape[dim] // parts).reshape([-1 if axis == dim else 1 for axis in range(len(shape))])
    return level


def routed_block(stream_key, own, number, rows, amount, top, reach, slope):
    sequence = jax.random.permutation(stream_key, amount)
    heavy_load, ordinary = portions_of(amount, rows * top, reach, slope, True), portions_of(amount, rows * top, reach, slope, False)
    places = jnp.arange(amount)

    def named(lengths, rotation):
        used = int((lengths > 0).sum())
        fixed = max(1, used // 4)
        moved = fixed + (places - fixed + rotation * (used - fixed)) % max(1, amount - fixed)
        return jnp.zeros((amount,), jnp.int32).at[sequence[jnp.where(places < fixed, places, moved)]].set(jnp.asarray(lengths, jnp.int32))

    lengths = jnp.where(number % 4 == 0, named(heavy_load, number // 4), named(ordinary, number - number // 4 - 1))
    mixed = jax.random.permutation(jax.random.fold_in(own, 3), amount)
    source_of, receiver = mixed[0:amount // 2 * 2:2], mixed[1:amount // 2 * 2:2]
    slack = jnp.minimum(lengths[source_of] - 1, reach - lengths[receiver]) // 2
    slack = jnp.where((source_of == sequence[0]) | (receiver == sequence[0]) | (lengths[receiver] == 0), 0, jnp.maximum(slack, 0))
    moved = jax.random.randint(jax.random.fold_in(own, 4), (amount // 2,), 0, 1 << 20) % (slack + 1)
    lengths = lengths.at[source_of].add(-moved).at[receiver].add(moved)
    members = jnp.searchsorted(jnp.cumsum(lengths), jnp.arange(rows * top), side="right").astype(jnp.int32)
    table = members.reshape(top, rows).T
    table = table[jax.random.permutation(jax.random.fold_in(own, 1), rows)]
    rotation = jax.random.randint(jax.random.fold_in(own, 2), (rows, 1), 0, top)
    return jnp.take_along_axis(table, (jnp.arange(top)[None, :] + rotation) % top, axis=1)


def portions_of(amount, total, reach, lean, full):
    weights = [(1 << 20) // math.isqrt(standing ** lean) + 1 for standing in range(1, amount + 1)]
    largest = reach if full else min(reach, max(-(-total // amount), total * weights[0] // sum(weights)))
    least = 1 if total - largest >= amount - 1 else 0
    given, surplus = [largest] + [least] * (amount - 1), total - largest - least * (amount - 1)
    while surplus > 0:
        free = [i for i in range(1, amount) if given[i] < largest] or [i for i in range(1, amount) if given[i] < reach]
        whole, budget = sum([weights[i] for i in free]), surplus
        for i in free:
            addition = min(reach - given[i], max(1, budget * weights[i] // whole), surplus)
            given[i] = given[i] + addition
            surplus = surplus - addition
    return np.array(given)


def scatter_about(stream_key, shape, spread, reach, pieces=(), kind=jnp.bfloat16):
    values = spread * jax.random.normal(stream_key, shape, jnp.float32)
    if pieces:
        values = values * block_scale(stream_key, shape, pieces, -0.22, 0.18)
    return jnp.clip(values, -reach, reach).astype(kind)


def setup_inputs(seed: int = 0) -> dict:
    splits = jax.random.split(jax.random.key(seed), 13)
    fore_entry = scatter_about(splits[0], (N_PIPE, TOKENS, D), 1.0, 6.0, ((0, 16), (1, 16)))
    fore_feed = scatter_about(splits[1], (W - 1, TOKENS, D), 1.0, 6.0, ((1, 16),))
    fore_route_keys = jax.random.split(jax.random.fold_in(splits[2], 1), N_PIPE * W * TOKENS // TOK_DEV)
    fore_route_turns = jax.random.permutation(jax.random.fold_in(splits[2], 3), N_PIPE * W * TOKENS // TOK_DEV)
    fore_route = jax.vmap(lambda own, number: routed_block(jax.random.fold_in(splits[2], 2), own, number, TOK_DEV, EXPERTS, TOP, CAP, 2))(fore_route_keys, fore_route_turns).reshape((N_PIPE, W, TOKENS, TOP))
    fore_gate = jnp.clip(0.2 + 0.8 * jax.random.uniform(splits[3], (N_PIPE, W, TOKENS, TOP), jnp.float32) ** block_scale(splits[3], (N_PIPE, W, TOKENS, TOP), ((0, 16), (2, 16)), -0.2, 0.2), 0.2, 1.0)
    back_entry = scatter_about(splits[4], (N_PIPE, TOKENS, D), 1.0, 6.0, ((0, 16), (1, 16)))
    back_feed = scatter_about(splits[5], (W - 1, TOKENS, D), 1.0, 6.0, ((1, 16),))
    back_stash = scatter_about(splits[6], (N_PIPE, W, TOKENS, D), 1.0, 6.0, ((0, 16), (2, 16)))
    back_route_keys = jax.random.split(jax.random.fold_in(splits[7], 1), N_PIPE * W * TOKENS // TOK_DEV)
    back_route_turns = jax.random.permutation(jax.random.fold_in(splits[7], 3), N_PIPE * W * TOKENS // TOK_DEV)
    back_route = jax.vmap(lambda own, number: routed_block(jax.random.fold_in(splits[7], 2), own, number, TOK_DEV, EXPERTS, TOP, CAP, 2))(back_route_keys, back_route_turns).reshape((N_PIPE, W, TOKENS, TOP))
    back_gate = jnp.clip(0.2 + 0.8 * jax.random.uniform(splits[8], (N_PIPE, W, TOKENS, TOP), jnp.float32) ** block_scale(splits[8], (N_PIPE, W, TOKENS, TOP), ((0, 16), (2, 16)), -0.2, 0.2), 0.2, 1.0)
    w_gate = scatter_about(splits[9], (N_PIPE, D, EXPERTS * FF), D ** -0.5, 0.09375, ((0, 16), (2, 16)))
    w_up = scatter_about(splits[10], (N_PIPE, D, EXPERTS * FF), D ** -0.5, 0.09375, ((0, 16), (2, 16)))
    w_down = scatter_about(splits[11], (N_PIPE, EXPERTS * FF, D), FF ** -0.5, 0.1875, ((0, 16), (1, 16)))
    return {"fore_entry": fore_entry, "fore_feed": fore_feed, "fore_route": fore_route, "fore_gate": fore_gate, "back_entry": back_entry, "back_feed": back_feed, "back_stash": back_stash, "back_route": back_route, "back_gate": back_gate, "w_gate": w_gate, "w_up": w_up, "w_down": w_down}


def weight_map(route, gate):
    hit = (route[:, :, None] == jnp.arange(EXPERTS, dtype=jnp.int32)[None, None, :]).astype(jnp.float32)
    return jnp.sum(gate[:, :, None].astype(jnp.float32) * hit, axis=1)


def slice_of(w_gate_s, w_up_s, w_down_s, index):
    start = (index * HID).astype(jnp.int32)
    gate_cols = lax.dynamic_slice_in_dim(w_gate_s, start, HID, 1)
    up_cols = lax.dynamic_slice_in_dim(w_up_s, start, HID, 1)
    down_rows = lax.dynamic_slice_in_dim(w_down_s, start, HID, 0)
    return gate_cols, up_cols, down_rows


def owner_weight(weights, index):
    owner = ((index * HID) // FF).astype(jnp.int32)
    return lax.dynamic_slice_in_dim(weights, owner, 1, 1)


def forward_section(inputs):
    tokens, route, gate, w_gate_s, w_up_s, w_down_s = inputs
    weights = weight_map(route, gate)

    def add_slice(index, running):
        gate_cols, up_cols, down_rows = slice_of(w_gate_s, w_up_s, w_down_s, index)
        pre_gate = jnp.dot(tokens, gate_cols, preferred_element_type=jnp.float32)
        pre_up = jnp.dot(tokens, up_cols, preferred_element_type=jnp.float32)
        hidden = (jax.nn.silu(pre_gate) * pre_up).astype(jnp.bfloat16)
        partial_value = jnp.dot(hidden, down_rows, preferred_element_type=jnp.float32).astype(jnp.bfloat16)
        partial_value = lax.optimization_barrier(partial_value).astype(jnp.float32)
        return running + owner_weight(weights, index) * partial_value

    running = lax.fori_loop(0, N_EP, add_slice, jnp.zeros(tokens.shape, jnp.float32))
    return (tokens.astype(jnp.float32) + running).astype(jnp.bfloat16)


def backward_section(inputs):
    tokens, cotangent, route, gate, w_gate_s, w_up_s, w_down_s = inputs
    weights = weight_map(route, gate)

    def add_slice(index, running):
        gate_cols, up_cols, down_rows = slice_of(w_gate_s, w_up_s, w_down_s, index)
        pre_gate = jnp.dot(tokens, gate_cols, preferred_element_type=jnp.float32)
        pre_up = jnp.dot(tokens, up_cols, preferred_element_type=jnp.float32)
        grad_hidden = jnp.dot(cotangent, down_rows.T, preferred_element_type=jnp.float32)
        sigmoid = jax.nn.sigmoid(pre_gate)
        grad_gate = (grad_hidden * pre_up * sigmoid * (1.0 + pre_gate * (1.0 - sigmoid))).astype(jnp.bfloat16)
        grad_up = (grad_hidden * pre_gate * sigmoid).astype(jnp.bfloat16)
        grad_in = jnp.dot(grad_gate, gate_cols.T, preferred_element_type=jnp.float32) + jnp.dot(grad_up, up_cols.T, preferred_element_type=jnp.float32)
        grad_in = lax.optimization_barrier(grad_in.astype(jnp.bfloat16)).astype(jnp.float32)
        return running + owner_weight(weights, index) * grad_in

    running = lax.fori_loop(0, N_EP, add_slice, jnp.zeros(tokens.shape, jnp.float32))
    return (cotangent.astype(jnp.float32) + running).astype(jnp.bfloat16)


def reference(fore_entry, fore_feed, fore_route, fore_gate, back_entry, back_feed, back_stash, back_route, back_gate, w_gate, w_up, w_down):
    padding = jnp.zeros((1,) + fore_feed.shape[1:], fore_feed.dtype)
    fore_padded = jnp.concatenate([fore_feed, padding], axis=0)
    back_padded = jnp.concatenate([back_feed, padding], axis=0)

    def advance(current, moment):
        fore_in, back_in, fore_last, back_last = current
        fore_next = lax.map(forward_section, (fore_in, fore_route[:, moment], fore_gate[:, moment], w_gate, w_up, w_down))
        back_next = lax.map(backward_section, (back_stash[:, moment], back_in, back_route[:, moment], back_gate[:, moment], w_gate, w_up, w_down))
        fore_in = jnp.concatenate([fore_padded[moment][None], fore_next[:-1]], axis=0)
        back_in = jnp.concatenate([back_next[1:], back_padded[moment][None]], axis=0)
        return (fore_in, back_in, fore_next, back_next), None

    moments = jnp.arange(W, dtype=jnp.int32)
    start = (fore_entry, back_entry, fore_entry, back_entry)
    finals, unused = lax.scan(advance, start, moments)
    return finals[2], finals[3]
```

```python
import jax
import jax.numpy as jnp
from jax import lax
from jax.sharding import PartitionSpec as P

EXPERTS = 4
CAP = 40
FLAT = ("pipe", "ep")
FORE, BACK = 0, 1


def routing(mesh):
    sections = mesh.shape["pipe"]
    slices = mesh.shape["ep"] // EXPERTS

    def pairs(step):
        listed = []
        for s in range(sections):
            for x in range(EXPERTS):
                for y in range(slices):
                    ns, nx, ny = step(s, x, y)
                    source = (s * EXPERTS + x) * slices + y
                    target = ((ns % sections) * EXPERTS + nx % EXPERTS) * slices + ny % slices
                    listed.append((source, target))
        return listed

    def near(y):
        return y ^ 1

    def far(y):
        return slices - 1 - y

    return {
        "out": [pairs(lambda s, x, y, d=d: (s, x + d, y)) for d in range(EXPERTS)],
        "home": [pairs(lambda s, x, y, d=d: (s, x - d, y)) for d in range(EXPERTS)],
        "next": [
            [pairs(lambda s, x, y, d=d, by=by: (s + by, x + d, y)) for d in range(EXPERTS)]
            for by in (1, -1)
        ],
        "weights": pairs(lambda s, x, y: (s, x, near(y) if s % 2 == 0 else far(y))),
        "tokens": pairs(lambda s, x, y: (s, x, far(y) if s % 2 == 0 else near(y))),
    }


def places_of(ids, column, width):
    onehot = (ids[:, None] == jnp.arange(EXPERTS, dtype=jnp.int32)[None, :]).astype(jnp.int32)
    before = jnp.cumsum(onehot, axis=0) - onehot
    position = jnp.sum(before * onehot, axis=1)
    target = lax.rem(ids - column + EXPERTS, EXPERTS) * CAP + position
    return (
        target[None, None, :]
        == jnp.arange(EXPERTS * CAP, dtype=jnp.int32).reshape(EXPERTS, CAP, 1)
    )


def pack(tokens, places):
    return [
        jnp.dot(places[d], tokens, preferred_element_type=jnp.float32).astype(jnp.bfloat16)
        for d in range(EXPERTS)
    ]


def unpack(parts, places):
    rows = None
    for d in range(EXPERTS):
        term = lax.dot_general(
            places[d], parts[d], (((0,), (0,)), ((), ())), preferred_element_type=jnp.float32
        )
        rows = term if rows is None else rows + term
    return rows.astype(jnp.bfloat16)


def expert_forward(rows, weights):
    total = None
    for gate_cols, up_cols, down_rows in weights:
        pre_gate = jnp.dot(rows, gate_cols, preferred_element_type=jnp.float32)
        pre_up = jnp.dot(rows, up_cols, preferred_element_type=jnp.float32)
        hidden = (jax.nn.silu(pre_gate) * pre_up).astype(jnp.bfloat16)
        term = jnp.dot(hidden, down_rows, preferred_element_type=jnp.float32)
        total = term if total is None else total + term
    return total


def expert_backward(rows, cotangent, weights):
    contract = (((1,), (1,)), ((), ()))
    total = None
    for gate_cols, up_cols, down_rows in weights:
        pre_gate = jnp.dot(rows, gate_cols, preferred_element_type=jnp.float32)
        pre_up = jnp.dot(rows, up_cols, preferred_element_type=jnp.float32)
        grad_hidden = lax.dot_general(
            cotangent, down_rows, contract, preferred_element_type=jnp.float32
        )
        sigmoid = jax.nn.sigmoid(pre_gate)
        grad_gate = (grad_hidden * pre_up * sigmoid * (1.0 + pre_gate * (1.0 - sigmoid))).astype(
            jnp.bfloat16
        )
        grad_up = (grad_hidden * pre_gate * sigmoid).astype(jnp.bfloat16)
        term = lax.dot_general(grad_gate, gate_cols, contract, preferred_element_type=jnp.float32)
        term = term + lax.dot_general(
            grad_up, up_cols, contract, preferred_element_type=jnp.float32
        )
        total = term if total is None else total + term
    return total


def make_shards(mesh):
    table_of = routing(mesh)

    def send(value, pairs):
        return lax.ppermute(value, FLAT, pairs)

    def shards(
        fore_entry,
        fore_feed,
        fore_route,
        fore_gate,
        back_entry,
        back_feed,
        back_stash,
        back_route,
        back_gate,
        w_gate,
        w_up,
        w_down,
    ):
        section = lax.axis_index("pipe")
        sections = lax.axis_size("pipe")
        column = lax.axis_index("ep") // (lax.axis_size("ep") // EXPERTS)
        window = fore_route.shape[1]
        width = fore_route.shape[2]

        own_weights = (w_gate[0], w_up[0], w_down[0])
        other_weights = tuple(send(piece, table_of["weights"]) for piece in own_weights)
        weights = (own_weights, other_weights)

        table = jnp.stack(
            [
                jnp.stack([fore_route[0, :, :, 0].astype(jnp.float32), fore_gate[0, :, :, 0]], axis=1),
                jnp.stack([back_route[0, :, :, 0].astype(jnp.float32), back_gate[0, :, :, 0]], axis=1),
            ]
        )
        tables = [table] + [send(table, table_of["out"][d]) for d in range(1, EXPERTS)]
        ahead = [
            send(table[FORE, 1:, 0], table_of["next"][BACK][0]),
            send(table[BACK, 1:, 0], table_of["next"][FORE][0]),
        ]

        def places(direction, step):
            ids = table[direction, step, 0].astype(jnp.int32)
            return places_of(ids, column, width).astype(jnp.bfloat16)

        def next_places(direction, step):
            ids = ahead[direction][step].astype(jnp.int32)
            return places_of(ids, column, width).astype(jnp.bfloat16)

        def row_gates(direction, step):
            found = []
            for d in range(EXPERTS):
                ids = tables[d][direction, step, 0].astype(jnp.int32)
                here = places_of(ids, column, width)[0]
                gates = tables[d][direction, step, 1]
                found.append(jnp.sum(jnp.where(here, gates[None, :], 0.0), axis=1))
            return jnp.concatenate(found)[:, None]

        def dispatch(parts):
            return jnp.concatenate(
                [parts[0]] + [send(parts[d], table_of["out"][d]) for d in range(1, EXPERTS)]
            )

        def hand_on(parts, direction):
            return jnp.concatenate(
                [send(parts[d], table_of["next"][direction][d]) for d in range(EXPERTS)]
            )

        def go_home(rows):
            parts = rows.reshape(EXPERTS, CAP, rows.shape[1])
            return [parts[0]] + [
                send(parts[d], table_of["home"][d]) for d in range(1, EXPERTS)
            ]

        def swap(rows):
            return send(rows, table_of["tokens"])

        def finish(base, own, other, direction, step):
            added = row_gates(direction, step) * (own + other.astype(jnp.float32))
            return (base.astype(jnp.float32) + added).astype(jnp.bfloat16)

        fore_rows = dispatch(pack(fore_entry[0], places(FORE, 0)))
        back_rows = dispatch(pack(back_entry[0], places(BACK, 0)))
        outs = None
        for step in range(window):
            stash_rows = dispatch(pack(back_stash[0, step], places(BACK, step)))
            fore_other, stash_other, back_other = swap(fore_rows), swap(stash_rows), swap(back_rows)
            fore_back = swap(expert_forward(fore_other, weights).astype(jnp.bfloat16))
            fore_own = expert_forward(fore_rows, weights)
            fore_home = go_home(finish(fore_rows, fore_own, fore_back, FORE, step))
            back_back = swap(expert_backward(stash_other, back_other, weights).astype(jnp.bfloat16))
            back_own = expert_backward(stash_rows, back_rows, weights)
            back_home = go_home(finish(back_rows, back_own, back_back, BACK, step))
            fore_next = unpack(fore_home, places(FORE, step))
            back_next = unpack(back_home, places(BACK, step))
            if step == window - 1:
                outs = (fore_next[None], back_next[None])
            else:
                fore_next = jnp.where(section == sections - 1, fore_feed[step], fore_next)
                back_next = jnp.where(section == 0, back_feed[step], back_next)
                fore_rows = hand_on(pack(fore_next, next_places(FORE, step)), FORE)
                back_rows = hand_on(pack(back_next, next_places(BACK, step)), BACK)
        return outs

    return shards


def solution(mesh):
    return jax.shard_map(
        make_shards(mesh),
        mesh=mesh,
        in_specs=(
            P("pipe", "ep", None),
            P(None, "ep", None),
            P("pipe", None, "ep", None),
            P("pipe", None, "ep", None),
            P("pipe", "ep", None),
            P(None, "ep", None),
            P("pipe", None, "ep", None),
            P("pipe", None, "ep", None),
            P("pipe", None, "ep", None),
            P("pipe", None, "ep"),
            P("pipe", None, "ep"),
            P("pipe", "ep", None),
        ),
        out_specs=(P("pipe", "ep", None), P("pipe", "ep", None)),
        check_vma=False,
    )
```

```python
import functools
import jax
import jax.numpy as jnp
from jax import lax
from jax.experimental import pallas as pl
from jax.experimental.pallas import tpu as pltpu
from jax.sharding import PartitionSpec as P

EXPERTS = 4
CAP = 40
FLAT = ("pipe", "ep")
FORE, BACK = 0, 1
STRIP = 512
NT = (((1,), (1,)), ((), ()))
VMEM_LIMIT = 12 * 1024 * 1024
LITTLE = pl.CostEstimate(flops=1, bytes_accessed=1, transcendentals=0)


def routing(mesh):
    sections = mesh.shape["pipe"]
    slices = mesh.shape["ep"] // EXPERTS

    def pairs(step):
        listed = []
        for s in range(sections):
            for x in range(EXPERTS):
                for y in range(slices):
                    ns, nx, ny = step(s, x, y)
                    source = (s * EXPERTS + x) * slices + y
                    target = ((ns % sections) * EXPERTS + nx % EXPERTS) * slices + ny % slices
                    listed.append((source, target))
        return listed

    def near(y):
        return y ^ 1

    def far(y):
        return slices - 1 - y

    return {
        "out": [pairs(lambda s, x, y, d=d: (s, x + d, y)) for d in range(EXPERTS)],
        "home": [pairs(lambda s, x, y, d=d: (s, x - d, y)) for d in range(EXPERTS)],
        "next": [
            [pairs(lambda s, x, y, d=d, by=by: (s + by, x + d, y)) for d in range(EXPERTS)]
            for by in (1, -1)
        ],
        "weights": pairs(lambda s, x, y: (s, x, near(y) if s % 2 == 0 else far(y))),
        "tokens": pairs(lambda s, x, y: (s, x, far(y) if s % 2 == 0 else near(y))),
    }


def target_of(ids, column):
    tokens = ids.shape[1]
    lane = lax.broadcasted_iota(jnp.int32, (tokens, tokens), 1)
    sub = lax.broadcasted_iota(jnp.int32, (tokens, tokens), 0)
    earlier = (sub < lane).astype(jnp.bfloat16)
    hit = lax.broadcasted_iota(jnp.int32, (16, tokens), 0) == ids
    before = jnp.dot(hit.astype(jnp.bfloat16), earlier, preferred_element_type=jnp.float32)
    position = jnp.sum(jnp.where(hit, before, 0.0), axis=0, keepdims=True).astype(jnp.int32)
    away = ids - column
    away = jnp.where(away < 0, away + EXPERTS, away)
    return away * CAP + position


def as_column(row_values):
    size = row_values.shape[1]
    lane = lax.broadcasted_iota(jnp.int32, (size, size), 1)
    sub = lax.broadcasted_iota(jnp.int32, (size, size), 0)
    return jnp.sum(jnp.where(lane == sub, row_values, 0), axis=1, keepdims=True)


def packing(ids, column):
    target = target_of(ids, column)
    spot = lax.broadcasted_iota(jnp.int32, (CAP, ids.shape[1]), 0)
    return [(spot + d * CAP == target).astype(jnp.bfloat16) for d in range(EXPERTS)]


def unpacking(ids, column):
    target = as_column(target_of(ids, column))
    spot = lax.broadcasted_iota(jnp.int32, (ids.shape[1], CAP), 1)
    return [(spot + d * CAP == target).astype(jnp.bfloat16) for d in range(EXPERTS)]


def strips(width):
    step = STRIP if width % STRIP == 0 else width
    return [slice(start, start + step) for start in range(0, width, step)]


def column_index():
    return lax.axis_index("ep") // (lax.axis_size("ep") // EXPERTS)


def pack_kernel(picks, step, ids_ref, *refs):
    count = len(picks)
    sources, outs, held, sems = refs[:count], refs[count : count + EXPERTS], refs[-2], refs[-1]
    copies = [
        pltpu.make_async_copy(sources[k].at[picks[k]], held.at[k], sems.at[k]) for k in range(count)
    ]
    for copy in copies:
        copy.start()
    places = packing(ids_ref[step], column_index())
    width = held.shape[2]
    for k in range(count):
        copies[k].wait()
        for cols in strips(width):
            block = held[k, :, cols]
            goal = slice(cols.start + k * width, cols.stop + k * width)
            for d in range(EXPERTS):
                outs[d][:, goal] = jnp.dot(
                    places[d], block, preferred_element_type=jnp.float32
                ).astype(jnp.bfloat16)


def pick_rows(parts, pulls, cols):
    rows = jnp.dot(pulls[0], parts[0][:, cols], preferred_element_type=jnp.float32)
    for d in range(1, EXPERTS):
        rows = rows + jnp.dot(pulls[d], parts[d][:, cols], preferred_element_type=jnp.float32)
    return rows


def combine_kernel(step, ids_ref, gate_ref, base_ref, *refs):
    parts, out_ref = refs[:EXPERTS], refs[EXPERTS]
    pulls = unpacking(ids_ref[step], column_index())
    gates = as_column(gate_ref[step])
    for cols in strips(base_ref.shape[1]):
        rows = base_ref[:, cols].astype(jnp.float32) + gates * pick_rows(parts, pulls, cols)
        out_ref[:, cols] = rows.astype(jnp.bfloat16)


def relay_kernel(
    feeder, step, ids_ref, gate_ref, next_ref, base_ref, feed_ref, *refs
):
    parts, out_ref, outs = refs[:EXPERTS], refs[EXPERTS], refs[EXPERTS + 1 :]
    column = column_index()
    feeds = lax.axis_index("pipe") == feeder
    pulls = unpacking(ids_ref[step], column)
    places = packing(next_ref[step + 1], column)
    gates = as_column(gate_ref[step])
    for cols in strips(base_ref.shape[1]):
        rows = base_ref[:, cols].astype(jnp.float32) + gates * pick_rows(parts, pulls, cols)
        rows = jnp.where(feeds, feed_ref[:, cols].astype(jnp.float32), rows).astype(jnp.bfloat16)
        out_ref[:, cols] = rows
        for d in range(EXPERTS):
            outs[d][:, cols] = jnp.dot(
                places[d], rows, preferred_element_type=jnp.float32
            ).astype(jnp.bfloat16)


def finish_kernel(own_ref, other_ref, *outs):
    for cols in strips(own_ref.shape[1]):
        total = own_ref[:, cols] + other_ref[:, cols].astype(jnp.float32)
        for d in range(EXPERTS):
            outs[d][:, cols] = total[d * CAP : (d + 1) * CAP].astype(jnp.bfloat16)


def forward_kernel(x_ref, *refs):
    weights, out_ref = refs[:6], refs[6]
    x = x_ref[...]
    hidden = []
    for k in range(2):
        pre_gate = jnp.dot(x, weights[3 * k][...], preferred_element_type=jnp.float32)
        pre_up = jnp.dot(x, weights[3 * k + 1][...], preferred_element_type=jnp.float32)
        hidden.append((pre_gate * jax.nn.sigmoid(pre_gate) * pre_up).astype(jnp.bfloat16))
    for cols in strips(x_ref.shape[1]):
        total = jnp.dot(hidden[0], weights[2][:, cols], preferred_element_type=jnp.float32)
        total = total + jnp.dot(hidden[1], weights[5][:, cols], preferred_element_type=jnp.float32)
        out_ref[:, cols] = total.astype(out_ref.dtype)


def slope_kernel(x_ref, *refs):
    weights, out_refs = refs[:4], refs[4:6]
    x = x_ref[:, : weights[0].shape[0]]
    for k in range(2):
        pre_gate = jnp.dot(x, weights[2 * k][...], preferred_element_type=jnp.float32)
        pre_up = jnp.dot(x, weights[2 * k + 1][...], preferred_element_type=jnp.float32)
        sigmoid = jax.nn.sigmoid(pre_gate)
        span = pre_gate.shape[1]
        cols = slice(k * span, (k + 1) * span)
        out_refs[0][:, cols] = pre_up * sigmoid * (1.0 + pre_gate * (1.0 - sigmoid))
        out_refs[1][:, cols] = pre_gate * sigmoid


def backward_kernel(c_ref, gate_slope_ref, up_slope_ref, *refs):
    weights, out_ref = refs[:6], refs[6]
    width = out_ref.shape[1]
    cotangent = c_ref[:, c_ref.shape[1] - width :]
    grads = []
    for k in range(2):
        grad_hidden = lax.dot_general(
            cotangent, weights[k][...], NT, preferred_element_type=jnp.float32
        )
        span = grad_hidden.shape[1]
        cols = slice(k * span, (k + 1) * span)
        grads.append((grad_hidden * gate_slope_ref[:, cols]).astype(jnp.bfloat16))
        grads.append((grad_hidden * up_slope_ref[:, cols]).astype(jnp.bfloat16))
    for cols in strips(width):
        total = None
        for k in range(4):
            term = lax.dot_general(
                grads[k], weights[2 + k][cols], NT, preferred_element_type=jnp.float32
            )
            total = term if total is None else total + term
        out_ref[:, cols] = total.astype(out_ref.dtype)


def in_vmem(count):
    return [pl.BlockSpec(memory_space=pltpu.VMEM)] * count


def run_experts(kernel, rows, weights, outs):
    return pl.pallas_call(
        kernel,
        name=kernel.__name__,
        out_shape=outs,
        in_specs=in_vmem(len(rows) + len(weights)),
        out_specs=jax.tree.map(lambda _: pl.BlockSpec(memory_space=pltpu.VMEM), outs),
        compiler_params=pltpu.CompilerParams(vmem_limit_bytes=VMEM_LIMIT),
        cost_estimate=LITTLE,
    )(*rows, *weights)


def small_call(kernel, outs, specs):
    return pl.pallas_call(
        kernel,
        name=getattr(kernel, "func", kernel).__name__,
        out_shape=outs,
        in_specs=specs,
        out_specs=jax.tree.map(lambda _: pl.BlockSpec(memory_space=pltpu.VMEM), outs),
        compiler_params=pltpu.CompilerParams(vmem_limit_bytes=VMEM_LIMIT),
        cost_estimate=LITTLE,
    )


def tied(*values):
    return lax.optimization_barrier(values)


def make_shards(mesh):
    table_of = routing(mesh)

    def send(value, pairs):
        return lax.ppermute(value, FLAT, pairs)

    def shards(
        fore_entry,
        fore_feed,
        fore_route,
        fore_gate,
        back_entry,
        back_feed,
        back_stash,
        back_route,
        back_gate,
        w_gate,
        w_up,
        w_down,
    ):
        sections = lax.axis_size("pipe")
        window, tokens = fore_route.shape[1:3]
        width = fore_entry.shape[2]
        part = jax.ShapeDtypeStruct((CAP, width), jnp.bfloat16)
        whole = jax.ShapeDtypeStruct((tokens, width), jnp.bfloat16)

        own_weights = (w_gate[0], w_up[0], w_down[0])
        other_weights = tuple(send(piece, table_of["weights"]) for piece in own_weights)
        weights = (own_weights, other_weights)

        def in_rows(array):
            return array.reshape(window, 1, tokens)

        routes = (in_rows(fore_route), in_rows(back_route))
        gates = (in_rows(fore_gate), in_rows(back_gate))
        feeds = (fore_feed, back_feed)
        feeders = (sections - 1, 0)
        ahead = (
            send(routes[FORE], table_of["next"][BACK][0]),
            send(routes[BACK], table_of["next"][FORE][0]),
        )

        def pack(direction, step, picks, *arrays):
            count = len(arrays)
            piece = jax.ShapeDtypeStruct((CAP, width * count), jnp.bfloat16)
            return pl.pallas_call(
                functools.partial(pack_kernel, picks, step),
                name="pack_kernel",
                out_shape=[piece] * EXPERTS,
                in_specs=in_vmem(1) + [pl.BlockSpec(memory_space=pltpu.HBM)] * count,
                out_specs=in_vmem(EXPERTS),
                scratch_shapes=[
                    pltpu.VMEM((count, tokens, width), jnp.bfloat16),
                    pltpu.SemaphoreType.DMA((count,)),
                ],
                compiler_params=pltpu.CompilerParams(vmem_limit_bytes=VMEM_LIMIT),
                cost_estimate=LITTLE,
            )(routes[direction], *arrays)

        def relay(direction, step, base, parts):
            found = small_call(
                functools.partial(relay_kernel, feeders[direction], step),
                [whole] + [part] * EXPERTS,
                in_vmem(5 + EXPERTS),
            )(
                routes[direction],
                gates[direction],
                ahead[direction],
                base,
                feeds[direction][step],
                *parts,
            )
            return found[0], found[1:]

        def combine(direction, step, base, parts):
            return small_call(
                functools.partial(combine_kernel, step),
                whole,
                in_vmem(3 + EXPERTS),
            )(routes[direction], gates[direction], base, *parts)

        def finish(own, other):
            return small_call(
                finish_kernel, [part] * EXPERTS, in_vmem(2)
            )(own, other)

        def dispatch(parts):
            with jax.named_scope("dispatch"):
                return jnp.concatenate(
                    [parts[0]] + [send(parts[d], table_of["out"][d]) for d in range(1, EXPERTS)]
                )

        def hand_on(parts, direction):
            with jax.named_scope("hand_on"):
                return [send(parts[d], table_of["next"][direction][d]) for d in range(EXPERTS)]

        def go_home(parts):
            with jax.named_scope("go_home"):
                return [parts[0]] + [
                    send(parts[d], table_of["home"][d]) for d in range(1, EXPERTS)
                ]

        def swap(rows):
            with jax.named_scope("swap"):
                return send(rows, table_of["tokens"])

        def result(out_dtype):
            return jax.ShapeDtypeStruct((EXPERTS * CAP, width), out_dtype)

        def forward(rows, out_dtype):
            flat = [piece for group in weights for piece in group]
            return run_experts(forward_kernel, (rows,), flat, result(out_dtype))

        def slopes(rows):
            flat = [piece for group in weights for piece in group[:2]]
            hidden = sum(group[2].shape[0] for group in weights)
            out = jax.ShapeDtypeStruct((rows.shape[0], hidden), jnp.float32)
            return run_experts(slope_kernel, (rows,), flat, [out, out])

        def backward(cotangent, slope, out_dtype):
            flat = [group[2] for group in weights]
            flat = flat + [piece for group in weights for piece in group[:2]]
            return run_experts(backward_kernel, (cotangent, *slope), flat, result(out_dtype))

        pair_rows = dispatch(pack(BACK, 0, ((0, 0), (0,)), back_stash, back_entry))
        pair_rows, fore_entry = tied(pair_rows, fore_entry)
        fore_rows = dispatch(pack(FORE, 0, ((0,),), fore_entry))
        fore_base, back_base = fore_entry[0], back_entry[0]
        own_weights, other_weights = weights
        pair_rows, own_weights, other_weights, ahead = tied(
            pair_rows, own_weights, other_weights, ahead
        )
        weights = (own_weights, other_weights)

        pair_other = swap(pair_rows)
        fore_other = swap(fore_rows)
        fore_rows, back_stash = tied(fore_rows, back_stash)
        later_rows = dispatch(pack(BACK, 1, ((0, 1),), back_stash))
        back_out = backward(pair_other, slopes(pair_other), jnp.bfloat16)
        back_back = swap(back_out)
        pair_rows, later_rows, back_out = tied(pair_rows, later_rows, back_out)
        own_slope = slopes(pair_rows)
        back_own = backward(pair_rows, own_slope, jnp.float32)
        later_slope = slopes(later_rows)
        fore_other, back_own, later_slope = tied(fore_other, back_own, later_slope)
        fore_out = forward(fore_other, jnp.bfloat16)
        fore_back = swap(fore_out)
        fore_rows, fore_out = tied(fore_rows, fore_out)
        fore_own = forward(fore_rows, jnp.float32)
        later_rows, back_back, fore_own = tied(later_rows, back_back, fore_own)
        later_other = swap(later_rows)
        back_home = go_home(finish(back_own, back_back))
        fore_done = finish(fore_own, fore_back)
        fore_home = go_home(fore_done)
        back_home, fore_done = tied(back_home, fore_done)
        back_next, back_parts = relay(BACK, 0, back_base, back_home)
        back_parts = hand_on(back_parts, BACK)
        fore_home, back_parts[1] = tied(fore_home, back_parts[1])
        back_rows = jnp.concatenate(back_parts)
        fore_next, fore_parts = relay(FORE, 0, fore_base, fore_home)
        fore_rows = jnp.concatenate(hand_on(fore_parts, FORE))
        other_slope = slopes(later_other)

        back_other = swap(back_rows)
        fore_other = swap(fore_rows)
        back_base = send(back_next, table_of["next"][BACK][0])
        fore_base = send(fore_next, table_of["next"][FORE][0])
        back_other, fore_rows = tied(back_other, fore_rows)
        back_out = backward(back_other, other_slope, jnp.bfloat16)
        back_back = swap(back_out)
        back_rows, back_out = tied(back_rows, back_out)
        back_own = backward(back_rows, later_slope, jnp.float32)
        fore_other, back_own, back_base, fore_base = tied(
            fore_other, back_own, back_base, fore_base
        )
        fore_out = forward(fore_other, jnp.bfloat16)
        fore_back = swap(fore_out)
        fore_rows, fore_out = tied(fore_rows, fore_out)
        fore_own = forward(fore_rows, jnp.float32)
        back_back, fore_own = tied(back_back, fore_own)
        back_home = go_home(finish(back_own, back_back))
        fore_home = go_home(finish(fore_own, fore_back))
        back_base = combine(BACK, 1, back_base, back_home)
        fore_base = combine(FORE, 1, fore_base, fore_home)
        return fore_base[None], back_base[None]

    return shards


def solution(mesh):
    return jax.shard_map(
        make_shards(mesh),
        mesh=mesh,
        in_specs=(
            P("pipe", "ep", None),
            P(None, "ep", None),
            P("pipe", None, "ep", None),
            P("pipe", None, "ep", None),
            P("pipe", "ep", None),
            P(None, "ep", None),
            P("pipe", None, "ep", None),
            P("pipe", None, "ep", None),
            P("pipe", None, "ep", None),
            P("pipe", None, "ep"),
            P("pipe", None, "ep"),
            P("pipe", "ep", None),
        ),
        out_specs=(P("pipe", "ep", None), P("pipe", "ep", None)),
        check_vma=False,
    )
```

```python
import functools
import jax
import jax.numpy as jnp
from jax import lax
from jax.experimental import pallas as pl
from jax.experimental.pallas import tpu as pltpu
from jax.sharding import PartitionSpec as P

EXPERTS = 4
CAP = 40
FLAT = ("pipe", "ep")
FORE, BACK = 0, 1
STRIP = 512
NT = (((1,), (1,)), ((), ()))
VMEM_LIMIT = 12 * 1024 * 1024
LITTLE = pl.CostEstimate(flops=1, bytes_accessed=1, transcendentals=0)


def routing(mesh):
    sections = mesh.shape["pipe"]
    slices = mesh.shape["ep"] // EXPERTS

    def pairs(step):
        listed = []
        for s in range(sections):
            for x in range(EXPERTS):
                for y in range(slices):
                    ns, nx, ny = step(s, x, y)
                    source = (s * EXPERTS + x) * slices + y
                    target = ((ns % sections) * EXPERTS + nx % EXPERTS) * slices + ny % slices
                    listed.append((source, target))
        return listed

    def near(y):
        return y ^ 1

    def far(y):
        return slices - 1 - y

    return {
        "out": [pairs(lambda s, x, y, d=d: (s, x + d, y)) for d in range(EXPERTS)],
        "home": [pairs(lambda s, x, y, d=d: (s, x - d, y)) for d in range(EXPERTS)],
        "next": [
            [pairs(lambda s, x, y, d=d, by=by: (s + by, x + d, y)) for d in range(EXPERTS)]
            for by in (1, -1)
        ],
        "weights": pairs(lambda s, x, y: (s, x, near(y) if s % 2 == 0 else far(y))),
        "tokens": pairs(lambda s, x, y: (s, x, far(y) if s % 2 == 0 else near(y))),
    }


def target_of(ids, column):
    tokens = ids.shape[1]
    lane = lax.broadcasted_iota(jnp.int32, (tokens, tokens), 1)
    sub = lax.broadcasted_iota(jnp.int32, (tokens, tokens), 0)
    earlier = (sub < lane).astype(jnp.bfloat16)
    hit = lax.broadcasted_iota(jnp.int32, (16, tokens), 0) == ids
    before = jnp.dot(hit.astype(jnp.bfloat16), earlier, preferred_element_type=jnp.float32)
    position = jnp.sum(jnp.where(hit, before, 0.0), axis=0, keepdims=True).astype(jnp.int32)
    away = ids - column
    away = jnp.where(away < 0, away + EXPERTS, away)
    return away * CAP + position


def as_column(row_values):
    size = row_values.shape[1]
    lane = lax.broadcasted_iota(jnp.int32, (size, size), 1)
    sub = lax.broadcasted_iota(jnp.int32, (size, size), 0)
    return jnp.sum(jnp.where(lane == sub, row_values, 0), axis=1, keepdims=True)


def packing(ids, column):
    target = target_of(ids, column)
    spot = lax.broadcasted_iota(jnp.int32, (CAP, ids.shape[1]), 0)
    return [(spot + d * CAP == target).astype(jnp.bfloat16) for d in range(EXPERTS)]


def unpacking(ids, column):
    target = as_column(target_of(ids, column))
    spot = lax.broadcasted_iota(jnp.int32, (ids.shape[1], CAP), 1)
    return [(spot + d * CAP == target).astype(jnp.bfloat16) for d in range(EXPERTS)]


def strips(width):
    step = STRIP if width % STRIP == 0 else width
    return [slice(start, start + step) for start in range(0, width, step)]


def column_index():
    return lax.axis_index("ep") // (lax.axis_size("ep") // EXPERTS)


def pack_kernel(picks, step, ids_ref, *refs):
    count = len(picks)
    sources, outs, held, sems = refs[:count], refs[count : count + EXPERTS], refs[-2], refs[-1]
    copies = [
        pltpu.make_async_copy(sources[k].at[picks[k]], held.at[k], sems.at[k]) for k in range(count)
    ]
    for copy in copies:
        copy.start()
    places = packing(ids_ref[step], column_index())
    width = held.shape[2]
    for k in range(count):
        copies[k].wait()
        for cols in strips(width):
            block = held[k, :, cols]
            goal = slice(cols.start + k * width, cols.stop + k * width)
            for d in range(EXPERTS):
                outs[d][:, goal] = jnp.dot(
                    places[d], block, preferred_element_type=jnp.float32
                ).astype(jnp.bfloat16)


def pick_rows(parts, pulls, cols):
    rows = jnp.dot(pulls[0], parts[0][:, cols], preferred_element_type=jnp.float32)
    for d in range(1, EXPERTS):
        rows = rows + jnp.dot(pulls[d], parts[d][:, cols], preferred_element_type=jnp.float32)
    return rows


def combine_kernel(step, ids_ref, gate_ref, base_ref, *refs):
    parts, out_ref = refs[:EXPERTS], refs[EXPERTS]
    pulls = unpacking(ids_ref[step], column_index())
    gates = as_column(gate_ref[step])
    for cols in strips(base_ref.shape[1]):
        rows = base_ref[:, cols].astype(jnp.float32) + gates * pick_rows(parts, pulls, cols)
        out_ref[:, cols] = rows.astype(jnp.bfloat16)


def relay_kernel(
    feeder, step, ids_ref, gate_ref, next_ref, base_ref, feed_ref, *refs
):
    parts, out_ref, outs = refs[:EXPERTS], refs[EXPERTS], refs[EXPERTS + 1 :]
    column = column_index()
    feeds = lax.axis_index("pipe") == feeder
    pulls = unpacking(ids_ref[step], column)
    places = packing(next_ref[step + 1], column)
    gates = as_column(gate_ref[step])
    for cols in strips(base_ref.shape[1]):
        rows = base_ref[:, cols].astype(jnp.float32) + gates * pick_rows(parts, pulls, cols)
        rows = jnp.where(feeds, feed_ref[:, cols].astype(jnp.float32), rows).astype(jnp.bfloat16)
        out_ref[:, cols] = rows
        for d in range(EXPERTS):
            outs[d][:, cols] = jnp.dot(
                places[d], rows, preferred_element_type=jnp.float32
            ).astype(jnp.bfloat16)


def finish_kernel(own_ref, other_ref, *outs):
    for cols in strips(own_ref.shape[1]):
        total = own_ref[:, cols] + other_ref[:, cols].astype(jnp.float32)
        for d in range(EXPERTS):
            outs[d][:, cols] = total[d * CAP : (d + 1) * CAP].astype(jnp.bfloat16)


def forward_kernel(x_ref, *refs):
    weights, out_ref = refs[:6], refs[6]
    x = x_ref[...]
    hidden = []
    for k in range(2):
        pre_gate = jnp.dot(x, weights[3 * k][...], preferred_element_type=jnp.float32)
        pre_up = jnp.dot(x, weights[3 * k + 1][...], preferred_element_type=jnp.float32)
        hidden.append((pre_gate * jax.nn.sigmoid(pre_gate) * pre_up).astype(jnp.bfloat16))
    for cols in strips(x_ref.shape[1]):
        total = jnp.dot(hidden[0], weights[2][:, cols], preferred_element_type=jnp.float32)
        total = total + jnp.dot(hidden[1], weights[5][:, cols], preferred_element_type=jnp.float32)
        out_ref[:, cols] = total.astype(out_ref.dtype)


def slope_kernel(x_ref, *refs):
    weights, out_refs = refs[:4], refs[4:6]
    x = x_ref[:, : weights[0].shape[0]]
    for k in range(2):
        pre_gate = jnp.dot(x, weights[2 * k][...], preferred_element_type=jnp.float32)
        pre_up = jnp.dot(x, weights[2 * k + 1][...], preferred_element_type=jnp.float32)
        sigmoid = jax.nn.sigmoid(pre_gate)
        span = pre_gate.shape[1]
        cols = slice(k * span, (k + 1) * span)
        out_refs[0][:, cols] = pre_up * sigmoid * (1.0 + pre_gate * (1.0 - sigmoid))
        out_refs[1][:, cols] = pre_gate * sigmoid


def backward_kernel(c_ref, gate_slope_ref, up_slope_ref, *refs):
    weights, out_ref = refs[:6], refs[6]
    width = out_ref.shape[1]
    cotangent = c_ref[:, c_ref.shape[1] - width :]
    grads = []
    for k in range(2):
        grad_hidden = lax.dot_general(
            cotangent, weights[k][...], NT, preferred_element_type=jnp.float32
        )
        span = grad_hidden.shape[1]
        cols = slice(k * span, (k + 1) * span)
        grads.append((grad_hidden * gate_slope_ref[:, cols]).astype(jnp.bfloat16))
        grads.append((grad_hidden * up_slope_ref[:, cols]).astype(jnp.bfloat16))
    for cols in strips(width):
        total = None
        for k in range(4):
            term = lax.dot_general(
                grads[k], weights[2 + k][cols], NT, preferred_element_type=jnp.float32
            )
            total = term if total is None else total + term
        out_ref[:, cols] = total.astype(out_ref.dtype)


def in_vmem(count):
    return [pl.BlockSpec(memory_space=pltpu.VMEM)] * count


def run_experts(kernel, rows, weights, outs):
    return pl.pallas_call(
        kernel,
        name=kernel.__name__,
        out_shape=outs,
        in_specs=in_vmem(len(rows) + len(weights)),
        out_specs=jax.tree.map(lambda _: pl.BlockSpec(memory_space=pltpu.VMEM), outs),
        compiler_params=pltpu.CompilerParams(vmem_limit_bytes=VMEM_LIMIT),
        cost_estimate=LITTLE,
    )(*rows, *weights)


def small_call(kernel, outs, specs):
    return pl.pallas_call(
        kernel,
        name=getattr(kernel, "func", kernel).__name__,
        out_shape=outs,
        in_specs=specs,
        out_specs=jax.tree.map(lambda _: pl.BlockSpec(memory_space=pltpu.VMEM), outs),
        compiler_params=pltpu.CompilerParams(vmem_limit_bytes=VMEM_LIMIT),
        cost_estimate=LITTLE,
    )


def tied(*values):
    return lax.optimization_barrier(values)


def make_shards(mesh):
    table_of = routing(mesh)

    def send(value, pairs):
        return lax.ppermute(value, FLAT, pairs)

    def shards(
        fore_entry,
        fore_feed,
        fore_route,
        fore_gate,
        back_entry,
        back_feed,
        back_stash,
        back_route,
        back_gate,
        w_gate,
        w_up,
        w_down,
    ):
        sections = lax.axis_size("pipe")
        window, tokens = fore_route.shape[1:3]
        width = fore_entry.shape[2]
        part = jax.ShapeDtypeStruct((CAP, width), jnp.bfloat16)
        whole = jax.ShapeDtypeStruct((tokens, width), jnp.bfloat16)

        own_weights = (w_gate[0], w_up[0], w_down[0])
        other_weights = tuple(send(piece, table_of["weights"]) for piece in own_weights)
        weights = (own_weights, other_weights)

        def in_rows(array):
            return array.reshape(window, 1, tokens)

        routes = (in_rows(fore_route), in_rows(back_route))
        gates = (in_rows(fore_gate), in_rows(back_gate))
        feeds = (fore_feed, back_feed)
        feeders = (sections - 1, 0)
        ahead = (
            send(routes[FORE], table_of["next"][BACK][0]),
            send(routes[BACK], table_of["next"][FORE][0]),
        )

        def pack(direction, step, picks, *arrays):
            count = len(arrays)
            piece = jax.ShapeDtypeStruct((CAP, width * count), jnp.bfloat16)
            return pl.pallas_call(
                functools.partial(pack_kernel, picks, step),
                name="pack_kernel",
                out_shape=[piece] * EXPERTS,
                in_specs=in_vmem(1) + [pl.BlockSpec(memory_space=pltpu.HBM)] * count,
                out_specs=in_vmem(EXPERTS),
                scratch_shapes=[
                    pltpu.VMEM((count, tokens, width), jnp.bfloat16),
                    pltpu.SemaphoreType.DMA((count,)),
                ],
                compiler_params=pltpu.CompilerParams(vmem_limit_bytes=VMEM_LIMIT),
                cost_estimate=LITTLE,
            )(routes[direction], *arrays)

        def relay(direction, step, base, parts):
            found = small_call(
                functools.partial(relay_kernel, feeders[direction], step),
                [whole] + [part] * EXPERTS,
                in_vmem(5 + EXPERTS),
            )(
                routes[direction],
                gates[direction],
                ahead[direction],
                base,
                feeds[direction][step],
                *parts,
            )
            return found[0], found[1:]

        def combine(direction, step, base, parts):
            return small_call(
                functools.partial(combine_kernel, step),
                whole,
                in_vmem(3 + EXPERTS),
            )(routes[direction], gates[direction], base, *parts)

        def finish(own, other):
            return small_call(
                finish_kernel, [part] * EXPERTS, in_vmem(2)
            )(own, other)

        def dispatch(parts):
            with jax.named_scope("dispatch"):
                return jnp.concatenate(
                    [parts[0]] + [send(parts[d], table_of["out"][d]) for d in range(1, EXPERTS)]
                )

        def hand_on(parts, direction):
            with jax.named_scope("hand_on"):
                return [send(parts[d], table_of["next"][direction][d]) for d in range(EXPERTS)]

        def go_home(parts):
            with jax.named_scope("go_home"):
                return [parts[0]] + [
                    send(parts[d], table_of["home"][d]) for d in range(1, EXPERTS)
                ]

        def swap(rows):
            with jax.named_scope("swap"):
                return send(rows, table_of["tokens"])

        def result(out_dtype):
            return jax.ShapeDtypeStruct((EXPERTS * CAP, width), out_dtype)

        def forward(rows, out_dtype):
            flat = [piece for group in weights for piece in group]
            return run_experts(forward_kernel, (rows,), flat, result(out_dtype))

        def slopes(rows):
            flat = [piece for group in weights for piece in group[:2]]
            hidden = sum(group[2].shape[0] for group in weights)
            out = jax.ShapeDtypeStruct((rows.shape[0], hidden), jnp.float32)
            return run_experts(slope_kernel, (rows,), flat, [out, out])

        def backward(cotangent, slope, out_dtype):
            flat = [group[2] for group in weights]
            flat = flat + [piece for group in weights for piece in group[:2]]
            return run_experts(backward_kernel, (cotangent, *slope), flat, result(out_dtype))

        pair_rows = dispatch(pack(BACK, 0, ((0, 0), (0,)), back_stash, back_entry))
        own_weights, other_weights = weights
        fore_entry, back_stash, own_weights, other_weights, ahead = tied(
            fore_entry, back_stash, own_weights, other_weights, ahead
        )
        weights = (own_weights, other_weights)
        fore_rows = dispatch(pack(FORE, 0, ((0,),), fore_entry))
        fore_base, back_base = fore_entry[0], back_entry[0]

        pair_other = swap(pair_rows)
        fore_other = swap(fore_rows)
        back_out = backward(pair_other, slopes(pair_other), jnp.bfloat16)
        back_back = swap(back_out)
        pair_rows, back_stash, back_out = tied(pair_rows, back_stash, back_out)
        later_rows = dispatch(pack(BACK, 1, ((0, 1),), back_stash))
        own_slope = slopes(pair_rows)
        back_own = backward(pair_rows, own_slope, jnp.float32)
        later_slope = slopes(later_rows)
        fore_other, back_own = tied(fore_other, back_own)
        fore_out = forward(fore_other, jnp.bfloat16)
        fore_back = swap(fore_out)
        fore_rows, fore_out = tied(fore_rows, fore_out)
        fore_own = forward(fore_rows, jnp.float32)
        later_rows, back_back, fore_own = tied(later_rows, back_back, fore_own)
        later_other = swap(later_rows)
        back_home = go_home(finish(back_own, back_back))
        fore_done = finish(fore_own, fore_back)
        fore_home = go_home(fore_done)
        back_home, fore_home[1] = tied(back_home, fore_home[1])
        back_next, back_parts = relay(BACK, 0, back_base, back_home)
        back_parts = hand_on(back_parts, BACK)
        fore_home, back_parts[1] = tied(fore_home, back_parts[1])
        back_rows = jnp.concatenate(back_parts)
        fore_next, fore_parts = relay(FORE, 0, fore_base, fore_home)
        fore_rows = jnp.concatenate(hand_on(fore_parts, FORE))
        other_slope = slopes(later_other)

        back_other = swap(back_rows)
        fore_other = swap(fore_rows)
        back_base = send(back_next, table_of["next"][BACK][0])
        fore_base = send(fore_next, table_of["next"][FORE][0])
        back_other, fore_rows = tied(back_other, fore_rows)
        back_out = backward(back_other, other_slope, jnp.bfloat16)
        back_back = swap(back_out)
        back_rows, back_out = tied(back_rows, back_out)
        back_own = backward(back_rows, later_slope, jnp.float32)
        fore_other, back_own, back_base, fore_base = tied(
            fore_other, back_own, back_base, fore_base
        )
        fore_out = forward(fore_other, jnp.bfloat16)
        fore_back = swap(fore_out)
        fore_rows, fore_out = tied(fore_rows, fore_out)
        fore_own = forward(fore_rows, jnp.float32)
        back_back, fore_own = tied(back_back, fore_own)
        back_home = go_home(finish(back_own, back_back))
        fore_home = go_home(finish(fore_own, fore_back))
        back_base = combine(BACK, 1, back_base, back_home)
        fore_base = combine(FORE, 1, fore_base, fore_home)
        return fore_base[None], back_base[None]

    return shards


def solution(mesh):
    return jax.shard_map(
        make_shards(mesh),
        mesh=mesh,
        in_specs=(
            P("pipe", "ep", None),
            P(None, "ep", None),
            P("pipe", None, "ep", None),
            P("pipe", None, "ep", None),
            P("pipe", "ep", None),
            P(None, "ep", None),
            P("pipe", None, "ep", None),
            P("pipe", None, "ep", None),
            P("pipe", None, "ep", None),
            P("pipe", None, "ep"),
            P("pipe", None, "ep"),
            P("pipe", "ep", None),
        ),
        out_specs=(P("pipe", "ep", None), P("pipe", "ep", None)),
        check_vma=False,
    )
```
